128 devices in a mesh: depth: 16 (over y, x), rows: 8 (over z, core).
Axes of the slice: x: 4, y: 4, z: 4, core: 2. Of those that a mesh axis runs over, the one named last changes fastest.
Arguments:
- coarse: bfloat16 [272, 128, 1024], P('depth', 'rows'), may hold values from -6 to 6
- detail: bfloat16 [512, 256, 2048], P('depth', 'rows'), may hold values from -3.59375 to 3.59375
- layout: int32 [2048], replicated, may hold values from 0 to 2047, each once
- view_order: int32 [16], replicated, may hold values from 0 to 15, as said below
Outputs:
- frame: float32 [4, 256, 2048], P(None, 'rows', 'depth')
The draws below stay inside these ranges and needn't reach their ends.
Inputs may be any that keep to these rules, and one draw needn't show every extreme that they name: layout is a permutation of the columns. view_order[b] is b xor one number below 16, the same for all bricks, so every aligned block of 2, 4, 8 ... bricks holds an aligned block of ranks.
All inputs are finite; a program needn't handle non-finite values.
Results may differ from the reference program's by a relative error of at most 0.0003.
Values may be sent and summed in bfloat16 or wider, within the bound.
No kernel may reach another device: no remote copies, remote signals or barrier semaphores. Data moves between devices by JAX's collectives and lax.ppermute only.
A program may use at most 192 MiB of HBM per device.

```python
import jax
import jax.numpy as jnp
from jax import lax

W = 2048
ZD = 32
H = 256
HC = 128
WC = 1024
ZC = 17
BRICKS = 16
ZALL = 512
ZCALL = 272


def draw_coarse(key, part):
    key = jax.random.fold_in(key, 5)
    offset_key, noise_key = jax.random.split(key)
    offsets = jax.random.uniform(offset_key, (BRICKS,), jnp.float32, -2.5, 2.5)
    noise = jnp.clip(jax.random.normal(noise_key, (ZCALL, HC, WC), jnp.float32), -3.0, 3.0)
    brick_of = jnp.arange(ZCALL, dtype=jnp.int32) // ZC
    shifted = noise + offsets[brick_of][:, None, None]
    return shifted.astype(jnp.bfloat16)


def draw_view_order(key, part):
    key = jax.random.fold_in(key, 11)
    flipper = jax.random.randint(key, (), 0, BRICKS)
    return jnp.bitwise_xor(jnp.arange(BRICKS, dtype=jnp.int32), flipper).astype(jnp.int32)


def block_scale(stream_key, dims, pieces, smallest, top_value):
    loudness, own = 1.0, jax.random.fold_in(stream_key, 6)
    for position, blocks in pieces:
        draws = jnp.exp(jax.random.uniform(jax.random.fold_in(own, position), (blocks,), jnp.float32, smallest / len(pieces), top_value / len(pieces)))
        loudness = loudness * jnp.repeat(draws, dims[position] // blocks).reshape([-1 if axis == position else 1 for axis in range(len(dims))])
    return loudness


def centred(stream_key, extent, deviation, limit, pieces=(), held_as=jnp.bfloat16):
    drawn = jax.random.normal(stream_key, extent, jnp.float32) * deviation
    if len(pieces) > 0:
        drawn = block_scale(stream_key, extent, pieces, -0.22, 0.18) * drawn
    return jnp.clip(drawn, min=-limit, max=limit).astype(held_as)


def setup_inputs(seed: int = 0) -> dict:
    streams_of = jax.random.split(jax.random.key(seed), 5)
    return {
        "coarse": draw_coarse(jax.random.fold_in(streams_of[4], 71), 0),
        "detail": centred(streams_of[1], (ZALL, H, W), 0.6, 3.59375, ((0, 16), (1, 8))),
        "layout": jax.random.permutation(streams_of[2], W).astype(jnp.int32),
        "view_order": draw_view_order(jax.random.fold_in(streams_of[4], 71), 0),
    }


def widen_cols(coarse_vals):
    next_cols = jnp.roll(coarse_vals, -1, axis=-1)
    midway = 0.5 * (coarse_vals + next_cols)
    return jnp.stack([coarse_vals, midway], axis=-1).reshape(coarse_vals.shape[:-1] + (2 * coarse_vals.shape[-1],))

def lengthen(coarse_vals, next_rows):
    midway = 0.5 * (coarse_vals + next_rows)
    return jnp.stack([coarse_vals, midway], axis=2).reshape((coarse_vals.shape[0], 2 * coarse_vals.shape[1], coarse_vals.shape[2]))

def deepen(coarse_vals):
    midway = 0.5 * (coarse_vals[:-1] + coarse_vals[1:])
    return jnp.stack([coarse_vals[:-1], midway], axis=1).reshape((2 * (coarse_vals.shape[0] - 1),) + coarse_vals.shape[1:])

def shade_brick(values, row_above, row_below, total_depth):
    grad_x = 0.5 * (jnp.roll(values, -1, axis=2) - jnp.roll(values, 1, axis=2))
    grad_y = 0.5 * (row_below - row_above)
    upper_plane = jnp.concatenate([values[1:], values[-1:]], 0)
    lower_plane = jnp.concatenate([values[:1], values[:-1]], 0)
    grad_z = 0.5 * (upper_plane - lower_plane)
    facing = jnp.abs(0.48 * grad_x + 0.6 * grad_y + 0.64 * grad_z)
    shading = 0.35 + 0.65 * facing / jnp.sqrt(1.0 + grad_x * grad_x + grad_y * grad_y + grad_z * grad_z)
    optical = 2.0 / total_depth * jax.nn.softplus(1.5 * values - 0.5)
    before = jnp.cumsum(optical, axis=0) - optical
    weight = jnp.exp(-before) * -jnp.expm1(-optical) * shading
    shaded = jnp.stack([lax.optimization_barrier(jnp.sum(weight * jax.nn.sigmoid(2.0 * values), 0)), lax.optimization_barrier(jnp.sum(weight * jax.nn.sigmoid(-values), 0)), lax.optimization_barrier(jnp.sum(weight * jnp.exp(-0.5 * values * values), 0))], 0)
    through = jnp.exp(-lax.optimization_barrier(jnp.sum(optical, 0)))
    return (shaded, through)

def reference(coarse, detail, layout, view_order):
    total_depth = ZD * BRICKS

    def one_brick(brick):
        brick_coarse = lax.dynamic_slice_in_dim(coarse, brick * ZC, ZC, 0).astype(jnp.float32)
        brick_detail = lax.dynamic_slice_in_dim(detail, brick * ZD, ZD, 0)
        widened = widen_cols(brick_coarse)
        lengthened = lengthen(widened, jnp.roll(widened, -1, axis=1))
        values = deepen(lengthened) + jnp.take(brick_detail, layout, axis=2).astype(jnp.float32)
        return shade_brick(values, jnp.roll(values, 1, axis=1), jnp.roll(values, -1, axis=1), total_depth)
    colors, throughs = lax.map(one_brick, jnp.arange(BRICKS, dtype=jnp.int32))
    sorted_ids = jnp.argsort(view_order).astype(jnp.int32)

    def composite(running, brick_id):
        accumulated, passing = running
        return ((accumulated + passing[None] * colors[brick_id], passing * throughs[brick_id]), None)
    start_vals = (jnp.zeros((3, H, W), jnp.float32), jnp.ones((H, W), jnp.float32))
    (accumulated, passing), _ = lax.scan(composite, start_vals, sorted_ids)
    return jnp.concatenate([accumulated, (1.0 - passing)[None]], 0)
```

```python
import functools
import math

import jax
import jax.numpy as jnp
from jax import lax
from jax.experimental import pallas as pl
from jax.experimental.pallas import tpu as pltpu
from jax.sharding import PartitionSpec as P

F32 = jnp.float32
BF16 = jnp.bfloat16
BLOCKS = 16
TILES = 8
PLANES = 32
PITCH = 40
CPITCH = 24
LOG2E = math.log2(math.e)
GAIN = 0.65 * 0.48
STEPS = 2048.0
COLOR_TOP = 32767.0
TAU_TOP = 32767.0 - 10 * 2048.0


def fit_weight():
    import numpy as np

    top = 0.0545
    k = np.cos(np.pi * (np.arange(64) + 0.5) / 64)
    o = (k + 1) * top / 2
    c = np.polynomial.chebyshev.chebfit(k, -np.expm1(-o) / o, 2)
    p = np.polynomial.chebyshev.cheb2poly(c)
    q = np.zeros(3)
    base = np.poly1d([2 / top, -1.0])
    poly = np.poly1d([0.0])
    for i, ci in enumerate(p):
        poly = poly + ci * base**i
    q[: len(poly.coeffs)] = poly.coeffs[::-1]
    kappa = math.log(2) / 256
    return tuple(float(q[i] * kappa ** (i + 1)) for i in range(3))


W0, W1, W2 = fit_weight()


def onehot(lay_ref, p_ref, t):
    lay = lay_ref[pl.ds(t, 1), :]
    hi = lay // 256
    lo = lay - hi * 256
    rows = lax.broadcasted_iota(jnp.int32, (256, 256), 0).astype(BF16)
    for a in range(8):
        key = jnp.where(hi == a, lo, -1).astype(BF16)
        p_ref[256 * a : 256 * a + 256, :] = jnp.where(rows == key, BF16(1), BF16(0))


def coarse_tile(t, coarse_ref, ctop_ref, cbot_ref, w_ref, c_ref, h_ref):
    k0 = pl.multiple_of(t * 128, 128)
    k1 = pl.multiple_of(jnp.where(t == 7, 0, t + 1) * 128, 128)

    def widened(ref):
        both = jnp.concatenate([ref[:, pl.ds(k0, 128)], ref[:, pl.ds(k1, 128)]], axis=1)
        return jnp.dot(both, w_ref[...], preferred_element_type=F32)

    own, top, bot = widened(coarse_ref), widened(ctop_ref), widened(cbot_ref)
    for b in range(2):
        cols = slice(128 * b, 128 * b + 128)
        for m in range(17):
            c_ref[b, CPITCH * m + 8 : CPITCH * m + 24, :] = own[16 * m : 16 * m + 16, cols]
        for m in range(0, 24, 8):
            c_ref[b, pl.ds(CPITCH * m + 7, 8, stride=CPITCH), :] = top[m : m + 8, cols]
            c_ref[b, pl.ds(CPITCH * (m + 1), 8, stride=CPITCH), :] = bot[m : m + 8, cols]
        for m in range(17):
            for a in range(2):
                near = c_ref[b, CPITCH * m + 8 + 8 * a : CPITCH * m + 16 + 8 * a, :]
                far = c_ref[b, CPITCH * m + 9 + 8 * a : CPITCH * m + 17 + 8 * a, :]
                h_ref[b, pl.ds(PITCH * m + 8 + 16 * a, 8, stride=2), :] = near + near
                h_ref[b, pl.ds(PITCH * m + 9 + 16 * a, 8, stride=2), :] = near + far
        for m in range(0, 24, 8):
            edge = c_ref[b, pl.ds(CPITCH * m + 7, 8, stride=CPITCH), :]
            first = c_ref[b, pl.ds(CPITCH * m + 8, 8, stride=CPITCH), :]
            last = c_ref[b, pl.ds(CPITCH * (m + 1), 8, stride=CPITCH), :]
            h_ref[b, pl.ds(PITCH * m + 7, 8, stride=PITCH), :] = edge + first
            h_ref[b, pl.ds(PITCH * (m + 1), 8, stride=PITCH), :] = last + last


def values_tile(t, d_ref, h_ref, v_ref):
    for b in range(2):
        block = 2 * t + b
        cols = slice(128 * b, 128 * b + 128)
        for z in range(PLANES):
            m, n = z // 2, (z + 1) // 2
            at = PITCH * z + 8
            for g in range(0, 32, 8):
                near = h_ref[b, PITCH * m + 8 + g : PITCH * m + 16 + g, :]
                far = near if n == m else h_ref[b, PITCH * n + 8 + g : PITCH * n + 16 + g, :]
                v_ref[block, at + g : at + g + 8, :] = d_ref[32 * z + g : 32 * z + g + 8, cols] + (near + far)
        for side, row in ((0, 7), (1, PITCH)):
            for odd in range(2):
                for m in range(0, 16, 8):
                    near = h_ref[b, pl.ds(PITCH * m + row, 8, stride=PITCH), :]
                    far = near if odd == 0 else h_ref[b, pl.ds(PITCH * (m + 1) + row, 8, stride=PITCH), :]
                    r = 1024 + 32 * side + 16 * odd + m
                    v_ref[block, pl.ds(PITCH * (2 * m + odd) + row, 8, stride=2 * PITCH), :] = d_ref[r : r + 8, cols] + (near + far)


def matmul_tile(a_ref, e_ref, p_ref, d_ref):
    d_ref[0:1024, :] = jnp.dot(a_ref[...], p_ref[...], preferred_element_type=F32)
    d_ref[1024:1088, :] = jnp.dot(e_ref[...], p_ref[...], preferred_element_type=F32)


def code(x, top):
    c = jnp.floor(jnp.log2(x) * STEPS + (top + 0.5))
    return jnp.minimum(jnp.maximum(c, -32768.0), 32767.0)


def march(v_ref, block, g):
    lane = lax.broadcasted_iota(jnp.int32, (8, 128), 1)
    first, last = lane == 0, lane == 127
    left = jnp.where(block == 0, BLOCKS - 1, block - 1)
    right = jnp.where(block == BLOCKS - 1, 0, block + 1)

    def load(of, z, off=0):
        at = PITCH * z + 8 + 8 * g + off
        return v_ref[of, at : at + 8, :]

    zero = jnp.zeros((8, 128), F32)
    c = prev = load(block, 0)
    through = zero + 1.0
    a0 = a1 = a2 = a3 = zero
    for z in range(PLANES):
        following = load(block, z + 1) if z + 1 < PLANES else c
        xp = pltpu.roll(jnp.where(first, load(right, z), c), 127, 1)
        xm = pltpu.roll(jnp.where(last, load(left, z), c), 1, 1)
        dx = xp - xm
        dy = load(block, z, 1) - load(block, z, -1)
        dz = following - prev
        along = dx + (0.6 / 0.48) * dy + (0.64 / 0.48) * dz
        square = (4.0 + dx * dx) + (dy * dy + dz * dz)
        shading = 0.35 / GAIN + jnp.abs(along) * lax.rsqrt(square)
        l = jnp.log2(1.0 + jnp.exp2(c * (1.5 * LOG2E) - 0.5 * LOG2E))
        weight = through * (l * (W0 + l * (W1 + l * W2)))
        through = through - weight
        ws = weight * shading
        a0 = a0 + ws
        a1 = a1 + ws * jnp.tanh(c)
        a2 = a2 + ws * jnp.tanh(0.5 * c)
        a3 = a3 + ws * jnp.exp2((c * c) * (-0.5 * LOG2E))
        prev, c = c, following
    return a0, a1, a2, a3, through


def march_block(v_ref, o_ref, block):
    for half in range(2):
        sets = []
        for g in (2 * half, 2 * half + 1):
            a0, a1, a2, a3, through = march(v_ref, block, g)
            sets.append(
                (
                    code((0.5 * GAIN) * (a0 + a1), COLOR_TOP),
                    code((0.5 * GAIN) * (a0 - a2), COLOR_TOP),
                    code(GAIN * a3, COLOR_TOP),
                    code(-jnp.log2(through), TAU_TOP),
                )
            )
        for i in range(4):
            both = jnp.concatenate([sets[0][i], sets[1][i]], 0)
            o_ref[block, i, 16 * half : 16 * half + 16, :] = both.astype(jnp.int32).astype(jnp.int16)


def brick_kernel(a_ref, e_ref, coarse_ref, ctop_ref, cbot_ref, w_ref, lay_ref, o_ref, v_ref, p_ref, d_ref, c_ref, h_ref):
    def finish(t):
        coarse_tile(t, coarse_ref, ctop_ref, cbot_ref, w_ref, c_ref, h_ref)
        values_tile(t, d_ref, h_ref, v_ref)

    def early(i, _):
        t = jnp.where(i == 0, TILES - 1, 0)
        onehot(lay_ref, p_ref, t)
        matmul_tile(a_ref, e_ref, p_ref, d_ref)
        finish(t)
        return 0

    lax.fori_loop(0, 2, early, 0)
    onehot(lay_ref, p_ref, 1)

    def step(s, _):
        matmul_tile(a_ref, e_ref, p_ref, d_ref)
        march_block(v_ref, o_ref, jnp.where(s == 0, BLOCKS - 1, 2 * s - 1))
        march_block(v_ref, o_ref, 2 * s)
        finish(s + 1)
        onehot(lay_ref, p_ref, jnp.minimum(s + 2, TILES - 1))
        return 0

    lax.fori_loop(0, 6, step, 0)

    def late(s, _):
        march_block(v_ref, o_ref, 2 * s - 1)
        march_block(v_ref, o_ref, 2 * s)
        return 0

    lax.fori_loop(6, 8, late, 0)


def widening():
    import numpy as np

    w = np.zeros((256, 256), np.float32)
    for j in range(129):
        for x, part in ((2 * j, 0.25), (2 * j + 1, 0.125), (2 * j - 1, 0.125)):
            if 0 <= x < 256:
                w[j, x] = part
    return jnp.asarray(w, BF16)


VMEM = pl.BlockSpec(memory_space=pltpu.VMEM)


def brick(a, e, coarse, ctop, cbot, lay):
    return pl.pallas_call(
        brick_kernel,
        out_shape=jax.ShapeDtypeStruct((BLOCKS, 4, 32, 128), jnp.int16),
        in_specs=[VMEM] * 7,
        out_specs=VMEM,
        scratch_shapes=[
            pltpu.VMEM((BLOCKS, 33 * PITCH, 128), F32),
            pltpu.VMEM((2048, 256), BF16),
            pltpu.VMEM((1088, 256), F32),
            pltpu.VMEM((2, 25 * CPITCH, 128), F32),
            pltpu.VMEM((2, 25 * PITCH, 128), F32),
        ],
        compiler_params=pltpu.CompilerParams(vmem_limit_bytes=56 * 2**20),
        name="brick",
    )(a, e, coarse, ctop, cbot, widening(), lay)


def composite_kernel(order_ref, parts_ref, o_ref):
    flip = order_ref[0]

    def image(b, i):
        x = parts_ref[b, i].astype(jnp.int32).astype(F32)
        top = TAU_TOP if i == 3 else COLOR_TOP
        return jnp.where(x > -32768.0, jnp.exp2((x - top) * (1.0 / STEPS)), 0.0)

    tau = jnp.zeros((32, 128), F32)
    sums = [jnp.zeros((32, 128), F32) for _ in range(3)]
    for rank in range(BLOCKS):
        b = rank ^ flip
        passing = jnp.exp2(-tau)
        for i in range(3):
            sums[i] = sums[i] + passing * image(b, i)
        tau = tau + image(b, 3)
    for i in range(3):
        o_ref[i] = sums[i]
    o_ref[3] = 1.0 - jnp.exp2(-tau)


def composite(order, parts):
    return pl.pallas_call(
        composite_kernel,
        out_shape=jax.ShapeDtypeStruct((4, 32, 128), F32),
        in_specs=[pl.BlockSpec(memory_space=pltpu.SMEM), VMEM],
        out_specs=VMEM,
        name="composite",
    )(order, parts)


def edge(detail, coarse, row, crow):
    lines = detail[:, row, :]
    fine = jnp.concatenate([lines[0::2], lines[1::2]], 0)
    rough = jnp.pad(coarse[:, crow, :], ((0, 15), (0, 0)))
    return jnp.concatenate([fine, rough], 1)


def on_device(coarse, detail, layout, view_order):
    n = lax.axis_size("rows")
    above = lax.ppermute(edge(detail, coarse, 31, 15), "rows", [(i, (i + 1) % n) for i in range(n)])
    below = lax.ppermute(edge(detail, coarse, 0, 0), "rows", [((i + 1) % n, i) for i in range(n)])
    halo = jnp.concatenate([above[:, :2048], below[:, :2048]], 0)
    codes = brick(
        detail.reshape(1024, 2048), halo, coarse.reshape(272, 1024), above[:, 2048:], below[:, 2048:], layout.reshape(8, 256)
    )
    parts = lax.all_to_all(codes, "depth", 0, 0, tiled=True)
    return composite(view_order, parts)


def solution(mesh):
    in_specs = (P("depth", "rows", None), P("depth", "rows", None), P(), P())
    out_specs = P(None, "rows", "depth")
    return jax.shard_map(on_device, mesh=mesh, in_specs=in_specs, out_specs=out_specs, check_vma=False)
```

```python
import functools
import math

import jax
import jax.numpy as jnp
from jax import lax
from jax.experimental import pallas as pl
from jax.experimental.pallas import tpu as pltpu
from jax.sharding import PartitionSpec as P

F32 = jnp.float32
BF16 = jnp.bfloat16
BLOCKS = 16
TILES = 8
PLANES = 32
HALF = 544
PITCH = 40
CPITCH = 24
LOG2E = math.log2(math.e)
GAIN = 0.65 * 0.48
STEPS = 2048.0
COLOR_TOP = 32767.0
TAU_TOP = 32767.0 - 10 * 2048.0


def fit_weight():
    import numpy as np

    top = 0.0545
    k = np.cos(np.pi * (np.arange(64) + 0.5) / 64)
    o = (k + 1) * top / 2
    c = np.polynomial.chebyshev.chebfit(k, -np.expm1(-o) / o, 2)
    p = np.polynomial.chebyshev.cheb2poly(c)
    q = np.zeros(3)
    base = np.poly1d([2 / top, -1.0])
    poly = np.poly1d([0.0])
    for i, ci in enumerate(p):
        poly = poly + ci * base**i
    q[: len(poly.coeffs)] = poly.coeffs[::-1]
    kappa = math.log(2) / 256
    return tuple(float(q[i] * kappa ** (i + 1)) for i in range(3))


W0, W1, W2 = fit_weight()


def onehot(lay_ref, p_ref, at, t):
    lay = lay_ref[pl.ds(t, 1), :]
    hi = lay // 256
    lo = lay - hi * 256
    rows = lax.broadcasted_iota(jnp.int32, (256, 256), 0).astype(BF16)
    for a in range(8):
        key = jnp.where(hi == a, lo, -1).astype(BF16)
        p_ref[at, 256 * a : 256 * a + 256, :] = jnp.where(rows == key, BF16(1), BF16(0))


def coarse_tile(t, k_ref, w_ref, c_ref, h_ref):
    k0 = pl.multiple_of(t * 128, 128)
    k1 = pl.multiple_of((t + 1) % 8 * 128, 128)
    both = jnp.concatenate([k_ref[:, pl.ds(k0, 128)], k_ref[:, pl.ds(k1, 128)]], axis=1)
    wide = jnp.dot(both, w_ref[...], preferred_element_type=F32)
    own, top, bot = wide[:272], wide[272:304], wide[304:]
    for b in range(2):
        cols = slice(128 * b, 128 * b + 128)
        for m in range(17):
            c_ref[b, CPITCH * m + 8 : CPITCH * m + 24, :] = own[16 * m : 16 * m + 16, cols]
        for m in range(0, 24, 8):
            c_ref[b, pl.ds(CPITCH * m + 7, 8, stride=CPITCH), :] = top[m : m + 8, cols]
            c_ref[b, pl.ds(CPITCH * (m + 1), 8, stride=CPITCH), :] = bot[m : m + 8, cols]
        for m in range(17):
            for a in range(2):
                near = c_ref[b, CPITCH * m + 8 + 8 * a : CPITCH * m + 16 + 8 * a, :]
                far = c_ref[b, CPITCH * m + 9 + 8 * a : CPITCH * m + 17 + 8 * a, :]
                h_ref[b, pl.ds(PITCH * m + 8 + 16 * a, 8, stride=2), :] = near + near
                h_ref[b, pl.ds(PITCH * m + 9 + 16 * a, 8, stride=2), :] = near + far
        for m in range(0, 24, 8):
            edge = c_ref[b, pl.ds(CPITCH * m + 7, 8, stride=CPITCH), :]
            first = c_ref[b, pl.ds(CPITCH * m + 8, 8, stride=CPITCH), :]
            last = c_ref[b, pl.ds(CPITCH * (m + 1), 8, stride=CPITCH), :]
            h_ref[b, pl.ds(PITCH * m + 7, 8, stride=PITCH), :] = edge + first
            h_ref[b, pl.ds(PITCH * (m + 1), 8, stride=PITCH), :] = last + last


def local_terms(c):
    l = jnp.log2(1.0 + jnp.exp2(c * (1.5 * LOG2E) - 0.5 * LOG2E))
    return l * (W0 + l * (W1 + l * W2)), jnp.tanh(c), jnp.tanh(0.5 * c), jnp.exp2((c * c) * (-0.5 * LOG2E))


def values_tile(d_ref, h_ref, v_ref, e_refs):
    for b in range(2):
        cols = slice(128 * b, 128 * b + 128)
        for z in range(PLANES):
            m, n = z // 2, (z + 1) // 2
            at = PITCH * z + 8
            for g in range(0, 32, 8):
                near = h_ref[b, PITCH * m + 8 + g : PITCH * m + 16 + g, :]
                far = near if n == m else h_ref[b, PITCH * n + 8 + g : PITCH * n + 16 + g, :]
                c = d_ref[32 * z + g : 32 * z + g + 8, cols] + (near + far)
                v_ref[b, at + g : at + g + 8, :] = c
                if e_refs[b] is not None:
                    for i, term in enumerate(local_terms(c)):
                        e_refs[b][i, 32 * z + g : 32 * z + g + 8, :] = term
        for side, row in ((0, 7), (1, PITCH)):
            for odd in range(2):
                for m in range(0, 16, 8):
                    near = h_ref[b, pl.ds(PITCH * m + row, 8, stride=PITCH), :]
                    far = near if odd == 0 else h_ref[b, pl.ds(PITCH * (m + 1) + row, 8, stride=PITCH), :]
                    r = 1024 + 32 * side + 16 * odd + m
                    v_ref[b, pl.ds(PITCH * (2 * m + odd) + row, 8, stride=2 * PITCH), :] = d_ref[r : r + 8, cols] + (near + far)


def matmul_tile(a_ref, p_ref, at, d_ref):
    for r in (0, HALF):
        d_ref[r : r + HALF, :] = jnp.dot(a_ref[r : r + HALF, :], p_ref[at], preferred_element_type=F32)


def code(x, top):
    c = jnp.floor(jnp.log2(x) * STEPS + (top + 0.5))
    return jnp.minimum(jnp.maximum(c, -32768.0), 32767.0)


def march(trio, e_ref, groups):
    before, here, after = trio
    lane = lax.broadcasted_iota(jnp.int32, (8, 128), 1)
    first, last = lane == 0, lane == 127

    def load(of, g, z, off=0):
        at = PITCH * z + 8 + 8 * g + off
        return of[0][of[1], at : at + 8, :]

    zero = jnp.zeros((8, 128), F32)
    state = []
    for g in groups:
        c = load(here, g, 0)
        state.append((c, c, zero + 1.0, zero, zero, zero, zero))
    for z in range(PLANES):
        for at, g in enumerate(groups):
            prev, c, through, a0, a1, a2, a3 = state[at]
            following = load(here, g, z + 1) if z + 1 < PLANES else c
            xp = pltpu.roll(jnp.where(first, load(after, g, z), c), 127, 1)
            xm = pltpu.roll(jnp.where(last, load(before, g, z), c), 1, 1)
            dx = xp - xm
            dy = load(here, g, z, 1) - load(here, g, z, -1)
            dz = following - prev
            along = dx + (0.6 / 0.48) * dy + (0.64 / 0.48) * dz
            square = (4.0 + dx * dx) + (dy * dy + dz * dz)
            shading = 0.35 / GAIN + jnp.abs(along) * lax.rsqrt(square)
            absorbed, t1, t2, bell = (e_ref[i, 32 * z + 8 * g : 32 * z + 8 * g + 8, :] for i in range(4))
            weight = through * absorbed
            through = through - weight
            ws = weight * shading
            a0 = a0 + ws
            a1 = a1 + ws * t1
            a2 = a2 + ws * t2
            a3 = a3 + ws * bell
            state[at] = (c, following, through, a0, a1, a2, a3)
    return [one[2:] for one in state]


def march_half(trio, e_ref, o_ref, block, half):
    sets = []
    for through, a0, a1, a2, a3 in march(trio, e_ref, (2 * half, 2 * half + 1)):
        sets.append(
            (
                code((0.5 * GAIN) * (a0 + a1), COLOR_TOP),
                code((0.5 * GAIN) * (a0 - a2), COLOR_TOP),
                code(GAIN * a3, COLOR_TOP),
                code(-jnp.log2(through), TAU_TOP),
            )
        )
    for i in range(4):
        both = jnp.concatenate([sets[0][i], sets[1][i]], 0)
        o_ref[block, i, 16 * half : 16 * half + 16, :] = both.astype(jnp.int32).astype(jnp.int16)


def widening(w_ref):
    away = lax.broadcasted_iota(jnp.int32, (256, 256), 1) - 2 * lax.broadcasted_iota(jnp.int32, (256, 256), 0)
    w_ref[...] = jnp.where(away == 0, 0.25, jnp.where(jnp.abs(away) == 1, 0.125, 0.0)).astype(BF16)


def brick_kernel(a_hbm, above_hbm, below_hbm, coarse_hbm, lay_ref, o_ref, *scratch):
    a_ref, k_ref, w_ref, p_first, p_rest, d0, d1, d2, c0, c1, c2, h0, h1, h2, v0, v1, v2, v7 = scratch[:18]
    (e00, e01, e10, e11, e20, e21, e7), sem = scratch[18:25], scratch[25]
    cs, hs, ring, ds = (c0, c1, c2), (h0, h1, h2), (v0, v1, v2), (d0, d1, d2)
    es = ((e00, e01), (e10, e11), (e20, e21))
    copies = [
        pltpu.make_async_copy(of, to, sem.at[i])
        for i, (of, to) in enumerate(
            (
                (coarse_hbm, k_ref.at[pl.ds(0, 272)]),
                (above_hbm.at[:, pl.ds(2048, 1024)], k_ref.at[pl.ds(272, 32)]),
                (below_hbm.at[:, pl.ds(2048, 1024)], k_ref.at[pl.ds(304, 32)]),
                (a_hbm, a_ref.at[pl.ds(0, 1024)]),
                (above_hbm.at[:, pl.ds(0, 2048)], a_ref.at[pl.ds(1024, 32)]),
                (below_hbm.at[:, pl.ds(0, 2048)], a_ref.at[pl.ds(1056, 32)]),
            )
        )
    ]
    for copy in copies:
        copy.start()
    widening(w_ref)
    onehot(lay_ref, p_first, 0, TILES - 1)
    onehot(lay_ref, p_first, 1, 0)
    for copy in copies[:3]:
        copy.wait()
    coarse_tile(TILES - 1, k_ref, w_ref, c2, h2)
    coarse_tile(0, k_ref, w_ref, c0, h0)
    for copy in copies[3:]:
        copy.wait()
    matmul_tile(a_ref, p_first, 0, d0)
    matmul_tile(a_ref, p_first, 1, d1)
    for t in range(1, 7):
        onehot(lay_ref, p_rest, t - 1, t)
    values_tile(d0, h2, v7, (e7, None))
    values_tile(d0, h2, v2, (None, e21))
    matmul_tile(a_ref, p_rest, 0, d2)
    coarse_tile(1, k_ref, w_ref, c1, h1)
    values_tile(d1, h0, v0, es[0])

    def trios(prev, cur):
        return ((prev, 0), (prev, 1), (cur, 0)), ((prev, 1), (cur, 0), (cur, 1))

    def three(i, _):
        for j in range(3):
            s = 3 * i + j

            @pl.when(i < 2)
            def _(j=j, s=s):
                before, after = (j + 2) % 3, (j + 1) % 3
                one, two = trios(ring[before], ring[j])
                block = 2 * s - 1 if j else jnp.where(i == 0, BLOCKS - 1, 2 * s - 1)
                values_tile(ds[before], hs[after], ring[after], es[after])
                coarse_tile(jnp.minimum(s + 2, 7), k_ref, w_ref, cs[before], hs[before])
                matmul_tile(a_ref, p_rest, jnp.minimum(s + 1, 5), ds[j])
                march_half(one, es[before][1], o_ref, block, 0)
                march_half(one, es[before][1], o_ref, block, 1)
                march_half(two, es[j][0], o_ref, 2 * s, 0)
                march_half(two, es[j][0], o_ref, 2 * s, 1)

        return 0

    lax.fori_loop(0, 2, three, 0)
    for s, prev, cur, e_one, e_two in ((6, v2, v0, e21, e00), (7, v0, v7, e01, e7)):
        one, two = trios(prev, cur)
        for half in range(2):
            march_half(one, e_one, o_ref, 2 * s - 1, half)
            march_half(two, e_two, o_ref, 2 * s, half)


VMEM = pl.BlockSpec(memory_space=pltpu.VMEM)
ANY = pl.BlockSpec(memory_space=pl.ANY)


def brick(a, above, below, coarse, lay):
    return pl.pallas_call(
        brick_kernel,
        out_shape=jax.ShapeDtypeStruct((BLOCKS, 4, 32, 128), jnp.int16),
        in_specs=[ANY] * 4 + [VMEM],
        out_specs=VMEM,
        scratch_shapes=[
            pltpu.VMEM((1088, 2048), BF16),
            pltpu.VMEM((336, 1024), BF16),
            pltpu.VMEM((256, 256), BF16),
            pltpu.VMEM((2, 2048, 256), BF16),
            pltpu.VMEM((6, 2048, 256), BF16),
            *[pltpu.VMEM((1088, 256), F32)] * 3,
            *[pltpu.VMEM((2, 25 * CPITCH, 128), F32)] * 3,
            *[pltpu.VMEM((2, 25 * PITCH, 128), F32)] * 3,
            *[pltpu.VMEM((2, 33 * PITCH, 128), F32)] * 4,
            *[pltpu.VMEM((4, 1024, 128), F32)] * 7,
            pltpu.SemaphoreType.DMA((6,)),
        ],
        compiler_params=pltpu.CompilerParams(vmem_limit_bytes=58 * 2**20),
        name="brick",
    )(a, above, below, coarse, lay)


def composite_kernel(order_ref, parts_ref, o_ref):
    flip = order_ref[0]

    def image(b, i):
        x = parts_ref[b, i].astype(jnp.int32).astype(F32)
        top = TAU_TOP if i == 3 else COLOR_TOP
        return jnp.where(x > -32768.0, jnp.exp2((x - top) * (1.0 / STEPS)), 0.0)

    tau = jnp.zeros((32, 128), F32)
    sums = [jnp.zeros((32, 128), F32) for _ in range(3)]
    for rank in range(BLOCKS):
        b = rank ^ flip
        passing = jnp.exp2(-tau)
        for i in range(3):
            sums[i] = sums[i] + passing * image(b, i)
        tau = tau + image(b, 3)
    for i in range(3):
        o_ref[i] = sums[i]
    o_ref[3] = 1.0 - jnp.exp2(-tau)


def composite(order, parts):
    return pl.pallas_call(
        composite_kernel,
        out_shape=jax.ShapeDtypeStruct((4, 32, 128), F32),
        in_specs=[pl.BlockSpec(memory_space=pltpu.SMEM), VMEM],
        out_specs=VMEM,
        name="composite",
    )(order, parts)


def edge(detail, coarse, row, crow):
    lines = detail[:, row, :]
    fine = jnp.concatenate([lines[0::2], lines[1::2]], 0)
    rough = jnp.pad(coarse[:, crow, :], ((0, 15), (0, 0)))
    return jnp.concatenate([fine, rough], 1)


def on_device(coarse, detail, layout, view_order):
    n = lax.axis_size("rows")
    above = lax.ppermute(edge(detail, coarse, 31, 15), "rows", [(i, (i + 1) % n) for i in range(n)])
    below = lax.ppermute(edge(detail, coarse, 0, 0), "rows", [((i + 1) % n, i) for i in range(n)])
    codes = brick(detail.reshape(1024, 2048), above, below, coarse.reshape(272, 1024), layout.reshape(8, 256))
    parts = lax.all_to_all(codes, "depth", 0, 0, tiled=True)
    return composite(view_order, parts)


def solution(mesh):
    in_specs = (P("depth", "rows", None), P("depth", "rows", None), P(), P())
    out_specs = P(None, "rows", "depth")
    return jax.shard_map(on_device, mesh=mesh, in_specs=in_specs, out_specs=out_specs, check_vma=False)
```

```python
import functools
import math

import jax
import jax.numpy as jnp
from jax import lax
from jax.experimental import pallas as pl
from jax.experimental.pallas import tpu as pltpu
from jax.sharding import PartitionSpec as P

F32 = jnp.float32
BF16 = jnp.bfloat16
BLOCKS = 16
TILES = 8
PLANES = 32
HALF = 544
PITCH = 40
CPITCH = 24
LOG2E = math.log2(math.e)
GAIN = 0.65 * 0.48
STEPS = 2048.0
COLOR_TOP = 32767.0
TAU_TOP = 32767.0 - 10 * 2048.0


def fit_weight():
    import numpy as np

    top = 0.0545
    k = np.cos(np.pi * (np.arange(64) + 0.5) / 64)
    o = (k + 1) * top / 2
    c = np.polynomial.chebyshev.chebfit(k, -np.expm1(-o) / o, 2)
    p = np.polynomial.chebyshev.cheb2poly(c)
    q = np.zeros(3)
    base = np.poly1d([2 / top, -1.0])
    poly = np.poly1d([0.0])
    for i, ci in enumerate(p):
        poly = poly + ci * base**i
    q[: len(poly.coeffs)] = poly.coeffs[::-1]
    kappa = math.log(2) / 256
    return tuple(float(q[i] * kappa ** (i + 1)) for i in range(3))


W0, W1, W2 = fit_weight()


def onehot(lay_ref, p_ref, at, t):
    lay = lay_ref[pl.ds(t, 1), :]
    hi = lay // 256
    lo = lay - hi * 256
    rows = lax.broadcasted_iota(jnp.int32, (256, 256), 0).astype(BF16)
    for a in range(8):
        key = jnp.where(hi == a, lo, -1).astype(BF16)
        p_ref[at, 256 * a : 256 * a + 256, :] = jnp.where(rows == key, BF16(1), BF16(0))


def coarse_tile(t, k_ref, w_ref, c_ref, h_ref):
    k0 = pl.multiple_of(t * 128, 128)
    k1 = pl.multiple_of((t + 1) % 8 * 128, 128)
    both = jnp.concatenate([k_ref[:, pl.ds(k0, 128)], k_ref[:, pl.ds(k1, 128)]], axis=1)
    wide = jnp.dot(both, w_ref[...], preferred_element_type=F32)
    own, top, bot = wide[:272], wide[272:304], wide[304:]
    for b in range(2):
        cols = slice(128 * b, 128 * b + 128)
        for m in range(17):
            c_ref[b, CPITCH * m + 8 : CPITCH * m + 24, :] = own[16 * m : 16 * m + 16, cols]
        for m in range(0, 24, 8):
            c_ref[b, pl.ds(CPITCH * m + 7, 8, stride=CPITCH), :] = top[m : m + 8, cols]
            c_ref[b, pl.ds(CPITCH * (m + 1), 8, stride=CPITCH), :] = bot[m : m + 8, cols]
        for m in range(17):
            for a in range(2):
                near = c_ref[b, CPITCH * m + 8 + 8 * a : CPITCH * m + 16 + 8 * a, :]
                far = c_ref[b, CPITCH * m + 9 + 8 * a : CPITCH * m + 17 + 8 * a, :]
                h_ref[b, pl.ds(PITCH * m + 8 + 16 * a, 8, stride=2), :] = near + near
                h_ref[b, pl.ds(PITCH * m + 9 + 16 * a, 8, stride=2), :] = near + far
        for m in range(0, 24, 8):
            edge = c_ref[b, pl.ds(CPITCH * m + 7, 8, stride=CPITCH), :]
            first = c_ref[b, pl.ds(CPITCH * m + 8, 8, stride=CPITCH), :]
            last = c_ref[b, pl.ds(CPITCH * (m + 1), 8, stride=CPITCH), :]
            h_ref[b, pl.ds(PITCH * m + 7, 8, stride=PITCH), :] = edge + first
            h_ref[b, pl.ds(PITCH * (m + 1), 8, stride=PITCH), :] = last + last


def local_terms(c):
    l = jnp.log2(1.0 + jnp.exp2(c * (1.5 * LOG2E) - 0.5 * LOG2E))
    return l * (W0 + l * (W1 + l * W2)), jnp.tanh(c), jnp.tanh(0.5 * c), jnp.exp2((c * c) * (-0.5 * LOG2E))


def values_tile(d_ref, h_ref, v_ref, e_refs):
    for b in range(2):
        cols = slice(128 * b, 128 * b + 128)
        for z in range(PLANES):
            m, n = z // 2, (z + 1) // 2
            at = PITCH * z + 8
            for g in range(0, 32, 8):
                near = h_ref[b, PITCH * m + 8 + g : PITCH * m + 16 + g, :]
                far = near if n == m else h_ref[b, PITCH * n + 8 + g : PITCH * n + 16 + g, :]
                c = d_ref[32 * z + g : 32 * z + g + 8, cols] + (near + far)
                v_ref[b, at + g : at + g + 8, :] = c
                if e_refs[b] is not None:
                    for i, term in enumerate(local_terms(c)):
                        e_refs[b][i, 32 * z + g : 32 * z + g + 8, :] = term
        for side, row in ((0, 7), (1, PITCH)):
            for odd in range(2):
                for m in range(0, 16, 8):
                    near = h_ref[b, pl.ds(PITCH * m + row, 8, stride=PITCH), :]
                    far = near if odd == 0 else h_ref[b, pl.ds(PITCH * (m + 1) + row, 8, stride=PITCH), :]
                    r = 1024 + 32 * side + 16 * odd + m
                    v_ref[b, pl.ds(PITCH * (2 * m + odd) + row, 8, stride=2 * PITCH), :] = d_ref[r : r + 8, cols] + (near + far)


def matmul_tile(a_ref, p_ref, at, d_ref):
    for r in (0, HALF):
        d_ref[r : r + HALF, :] = jnp.dot(a_ref[r : r + HALF, :], p_ref[at], preferred_element_type=F32)


def code(x, top):
    c = jnp.floor(jnp.log2(x) * STEPS + (top + 0.5))
    return jnp.minimum(jnp.maximum(c, -32768.0), 32767.0)


def march(trio, e_ref, groups):
    before, here, after = trio
    lane = lax.broadcasted_iota(jnp.int32, (8, 128), 1)
    first, last = lane == 0, lane == 127

    def load(of, g, z, off=0):
        at = PITCH * z + 8 + 8 * g + off
        return of[0][of[1], at : at + 8, :]

    zero = jnp.zeros((8, 128), F32)
    state = []
    for g in groups:
        c = load(here, g, 0)
        state.append((c, c, zero + 1.0, zero, zero, zero, zero))
    for z in range(PLANES):
        for at, g in enumerate(groups):
            prev, c, through, a0, a1, a2, a3 = state[at]
            following = load(here, g, z + 1) if z + 1 < PLANES else c
            xp = pltpu.roll(jnp.where(first, load(after, g, z), c), 127, 1)
            xm = pltpu.roll(jnp.where(last, load(before, g, z), c), 1, 1)
            dx = xp - xm
            dy = load(here, g, z, 1) - load(here, g, z, -1)
            dz = following - prev
            along = dx + (0.6 / 0.48) * dy + (0.64 / 0.48) * dz
            square = (4.0 + dx * dx) + (dy * dy + dz * dz)
            shading = 0.35 / GAIN + jnp.abs(along) * lax.rsqrt(square)
            absorbed, t1, t2, bell = (e_ref[i, 32 * z + 8 * g : 32 * z + 8 * g + 8, :] for i in range(4))
            weight = through * absorbed
            through = through - weight
            ws = weight * shading
            a0 = a0 + ws
            a1 = a1 + ws * t1
            a2 = a2 + ws * t2
            a3 = a3 + ws * bell
            state[at] = (c, following, through, a0, a1, a2, a3)
    return [one[2:] for one in state]


def march_half(trio, e_ref, o_ref, block, half):
    sets = []
    for through, a0, a1, a2, a3 in march(trio, e_ref, (2 * half, 2 * half + 1)):
        sets.append(
            (
                code((0.5 * GAIN) * (a0 + a1), COLOR_TOP),
                code((0.5 * GAIN) * (a0 - a2), COLOR_TOP),
                code(GAIN * a3, COLOR_TOP),
                code(-jnp.log2(through), TAU_TOP),
            )
        )
    for i in range(4):
        both = jnp.concatenate([sets[0][i], sets[1][i]], 0)
        o_ref[block, i, 16 * half : 16 * half + 16, :] = both.astype(jnp.int32).astype(jnp.int16)


def widening(w_ref):
    away = lax.broadcasted_iota(jnp.int32, (256, 256), 1) - 2 * lax.broadcasted_iota(jnp.int32, (256, 256), 0)
    w_ref[...] = jnp.where(away == 0, 0.25, jnp.where(jnp.abs(away) == 1, 0.125, 0.0)).astype(BF16)


def brick_kernel(a_hbm, above_hbm, below_hbm, coarse_hbm, lay_hbm, o_hbm, *scratch):
    a_ref, k_ref, w_ref, p_first, p_rest, d0, d1, d2, c0, c1, c2, h0, h1, h2, v0, v1, v2, v7 = scratch[:18]
    (e00, e01, e10, e11, e20, e21, e7), lay_ref, o_ref, sem, o_sem = scratch[18:25], *scratch[25:]
    cs, hs, ring, ds = (c0, c1, c2), (h0, h1, h2), (v0, v1, v2), (d0, d1, d2)
    es = ((e00, e01), (e10, e11), (e20, e21))
    copies = [
        pltpu.make_async_copy(of, to, sem.at[i])
        for i, (of, to) in enumerate(
            (
                (lay_hbm, lay_ref),
                (coarse_hbm, k_ref.at[pl.ds(0, 272)]),
                (above_hbm.at[:, pl.ds(2048, 1024)], k_ref.at[pl.ds(272, 32)]),
                (below_hbm.at[:, pl.ds(2048, 1024)], k_ref.at[pl.ds(304, 32)]),
                (above_hbm.at[:, pl.ds(0, 2048)], a_ref.at[pl.ds(1024, 32)]),
                (below_hbm.at[:, pl.ds(0, 2048)], a_ref.at[pl.ds(1056, 32)]),
                (a_hbm.at[:, pl.ds(0, 1024)], a_ref.at[pl.ds(0, 1024), pl.ds(0, 1024)]),
                (a_hbm.at[:, pl.ds(1024, 1024)], a_ref.at[pl.ds(0, 1024), pl.ds(1024, 1024)]),
            )
        )
    ]
    for copy in copies:
        copy.start()
    widening(w_ref)
    copies[0].wait()
    onehot(lay_ref, p_first, 0, TILES - 1)
    onehot(lay_ref, p_first, 1, 0)
    for copy in copies[1:4]:
        copy.wait()
    coarse_tile(TILES - 1, k_ref, w_ref, c2, h2)
    coarse_tile(0, k_ref, w_ref, c0, h0)
    for copy in copies[4:7]:
        copy.wait()
    for r in (0, HALF):
        d0[r : r + HALF, :] = jnp.dot(a_ref[r : r + HALF, :1024], p_first[0, :1024, :], preferred_element_type=F32)
    copies[7].wait()
    for r in (0, HALF):
        d0[r : r + HALF, :] += jnp.dot(a_ref[r : r + HALF, 1024:], p_first[0, 1024:, :], preferred_element_type=F32)
    matmul_tile(a_ref, p_first, 1, d1)
    for t in range(1, 7):
        onehot(lay_ref, p_rest, t - 1, t)
    values_tile(d0, h2, v7, (e7, None))
    values_tile(d0, h2, v2, (None, e21))
    matmul_tile(a_ref, p_rest, 0, d2)
    coarse_tile(1, k_ref, w_ref, c1, h1)
    values_tile(d1, h0, v0, es[0])

    def leave(block):
        return pltpu.make_async_copy(o_ref.at[block], o_hbm.at[block], o_sem.at[block])

    def trios(prev, cur):
        return ((prev, 0), (prev, 1), (cur, 0)), ((prev, 1), (cur, 0), (cur, 1))

    def three(i, _):
        for j in range(3):
            s = 3 * i + j

            @pl.when(i < 2)
            def _(j=j, s=s):
                before, after = (j + 2) % 3, (j + 1) % 3
                one, two = trios(ring[before], ring[j])
                block = 2 * s - 1 if j else jnp.where(i == 0, BLOCKS - 1, 2 * s - 1)
                values_tile(ds[before], hs[after], ring[after], es[after])
                coarse_tile(jnp.minimum(s + 2, 7), k_ref, w_ref, cs[before], hs[before])
                matmul_tile(a_ref, p_rest, jnp.minimum(s + 1, 5), ds[j])
                march_half(one, es[before][1], o_ref, block, 0)
                march_half(one, es[before][1], o_ref, block, 1)
                leave(block).start()
                march_half(two, es[j][0], o_ref, 2 * s, 0)
                march_half(two, es[j][0], o_ref, 2 * s, 1)
                leave(2 * s).start()

        return 0

    lax.fori_loop(0, 2, three, 0)
    for s, prev, cur, e_one, e_two in ((6, v2, v0, e21, e00), (7, v0, v7, e01, e7)):
        one, two = trios(prev, cur)
        for half in range(2):
            march_half(one, e_one, o_ref, 2 * s - 1, half)
        leave(2 * s - 1).start()
        for half in range(2):
            march_half(two, e_two, o_ref, 2 * s, half)
        leave(2 * s).start()
    for block in range(BLOCKS):
        leave(block).wait()


VMEM = pl.BlockSpec(memory_space=pltpu.VMEM)
ANY = pl.BlockSpec(memory_space=pl.ANY)


def brick(a, above, below, coarse, lay):
    return pl.pallas_call(
        brick_kernel,
        out_shape=jax.ShapeDtypeStruct((BLOCKS, 4, 32, 128), jnp.int16),
        in_specs=[ANY] * 5,
        out_specs=ANY,
        scratch_shapes=[
            pltpu.VMEM((1088, 2048), BF16),
            pltpu.VMEM((336, 1024), BF16),
            pltpu.VMEM((256, 256), BF16),
            pltpu.VMEM((2, 2048, 256), BF16),
            pltpu.VMEM((6, 2048, 256), BF16),
            *[pltpu.VMEM((1088, 256), F32)] * 3,
            *[pltpu.VMEM((2, 25 * CPITCH, 128), F32)] * 3,
            *[pltpu.VMEM((2, 25 * PITCH, 128), F32)] * 3,
            *[pltpu.VMEM((2, 33 * PITCH, 128), F32)] * 4,
            *[pltpu.VMEM((4, 1024, 128), F32)] * 7,
            pltpu.VMEM((8, 256), jnp.int32),
            pltpu.VMEM((BLOCKS, 4, 32, 128), jnp.int16),
            pltpu.SemaphoreType.DMA((8,)),
            pltpu.SemaphoreType.DMA((BLOCKS,)),
        ],
        compiler_params=pltpu.CompilerParams(vmem_limit_bytes=63 * 2**20),
        name="brick",
    )(a, above, below, coarse, lay)


def composite_kernel(order_ref, parts_ref, o_ref):
    flip = order_ref[0]

    def image(b, i):
        x = parts_ref[b, i].astype(jnp.int32).astype(F32)
        top = TAU_TOP if i == 3 else COLOR_TOP
        return jnp.where(x > -32768.0, jnp.exp2((x - top) * (1.0 / STEPS)), 0.0)

    tau = jnp.zeros((32, 128), F32)
    sums = [jnp.zeros((32, 128), F32) for _ in range(3)]
    for rank in range(BLOCKS):
        b = rank ^ flip
        passing = jnp.exp2(-tau)
        for i in range(3):
            sums[i] = sums[i] + passing * image(b, i)
        tau = tau + image(b, 3)
    for i in range(3):
        o_ref[i] = sums[i]
    o_ref[3] = 1.0 - jnp.exp2(-tau)


def composite(order, parts):
    return pl.pallas_call(
        composite_kernel,
        out_shape=jax.ShapeDtypeStruct((4, 32, 128), F32),
        in_specs=[pl.BlockSpec(memory_space=pltpu.SMEM), VMEM],
        out_specs=VMEM,
        name="composite",
    )(order, parts)


def edge(detail, coarse, row, crow):
    lines = detail[:, row, :]
    fine = jnp.concatenate([lines[0::2], lines[1::2]], 0)
    rough = jnp.pad(coarse[:, crow, :], ((0, 15), (0, 0)))
    return jnp.concatenate([fine, rough], 1)


def on_device(coarse, detail, layout, view_order):
    n = lax.axis_size("rows")
    above = lax.ppermute(edge(detail, coarse, 31, 15), "rows", [(i, (i + 1) % n) for i in range(n)])
    below = lax.ppermute(edge(detail, coarse, 0, 0), "rows", [((i + 1) % n, i) for i in range(n)])
    codes = brick(detail.reshape(1024, 2048), above, below, coarse.reshape(272, 1024), layout.reshape(8, 256))
    parts = lax.all_to_all(codes, "depth", 0, 0, tiled=True)
    return composite(view_order, parts)


def solution(mesh):
    in_specs = (P("depth", "rows", None), P("depth", "rows", None), P(), P())
    out_specs = P(None, "rows", "depth")
    return jax.shard_map(on_device, mesh=mesh, in_specs=in_specs, out_specs=out_specs, check_vma=False)
```

```python
import functools
import math

import jax
import jax.numpy as jnp
from jax import lax
from jax.experimental import pallas as pl
from jax.experimental.pallas import tpu as pltpu
from jax.sharding import PartitionSpec as P

F32 = jnp.float32
BF16 = jnp.bfloat16
BLOCKS = 16
TILES = 8
PLANES = 32
HALF = 544
PITCH = 40
CPITCH = 24
LOG2E = math.log2(math.e)
GAIN = 0.65 * 0.48
STEPS = 2048.0
COLOR_TOP = 32767.0
TAU_TOP = 32767.0 - 10 * 2048.0


def fit_weight():
    import numpy as np

    top = 0.0545
    k = np.cos(np.pi * (np.arange(64) + 0.5) / 64)
    o = (k + 1) * top / 2
    c = np.polynomial.chebyshev.chebfit(k, -np.expm1(-o) / o, 2)
    p = np.polynomial.chebyshev.cheb2poly(c)
    q = np.zeros(3)
    base = np.poly1d([2 / top, -1.0])
    poly = np.poly1d([0.0])
    for i, ci in enumerate(p):
        poly = poly + ci * base**i
    q[: len(poly.coeffs)] = poly.coeffs[::-1]
    kappa = math.log(2) / 256
    return tuple(float(q[i] * kappa ** (i + 1)) for i in range(3))


W0, W1, W2 = fit_weight()


def onehot(lay_ref, p_ref, at, t):
    lay = lay_ref[pl.ds(t, 1), :]
    hi = lay // 256
    lo = lay - hi * 256
    rows = lax.broadcasted_iota(jnp.int32, (256, 256), 0).astype(BF16)
    for a in range(8):
        key = jnp.where(hi == a, lo, -1).astype(BF16)
        p_ref[at, 256 * a : 256 * a + 256, :] = jnp.where(rows == key, BF16(1), BF16(0))


def coarse_tile(t, k_ref, w_ref, c_ref, h_ref):
    k0 = pl.multiple_of(t * 128, 128)
    k1 = pl.multiple_of((t + 1) % 8 * 128, 128)
    both = jnp.concatenate([k_ref[:, pl.ds(k0, 128)], k_ref[:, pl.ds(k1, 128)]], axis=1)
    wide = jnp.dot(both, w_ref[...], preferred_element_type=F32)
    own, top, bot = wide[:272], wide[272:304], wide[304:]
    for b in range(2):
        cols = slice(128 * b, 128 * b + 128)
        for m in range(17):
            c_ref[b, CPITCH * m + 8 : CPITCH * m + 24, :] = own[16 * m : 16 * m + 16, cols]
        for m in range(0, 24, 8):
            c_ref[b, pl.ds(CPITCH * m + 7, 8, stride=CPITCH), :] = top[m : m + 8, cols]
            c_ref[b, pl.ds(CPITCH * (m + 1), 8, stride=CPITCH), :] = bot[m : m + 8, cols]
        for m in range(17):
            for a in range(2):
                near = c_ref[b, CPITCH * m + 8 + 8 * a : CPITCH * m + 16 + 8 * a, :]
                far = c_ref[b, CPITCH * m + 9 + 8 * a : CPITCH * m + 17 + 8 * a, :]
                h_ref[b, pl.ds(PITCH * m + 8 + 16 * a, 8, stride=2), :] = near + near
                h_ref[b, pl.ds(PITCH * m + 9 + 16 * a, 8, stride=2), :] = near + far
        for m in range(0, 24, 8):
            edge = c_ref[b, pl.ds(CPITCH * m + 7, 8, stride=CPITCH), :]
            first = c_ref[b, pl.ds(CPITCH * m + 8, 8, stride=CPITCH), :]
            last = c_ref[b, pl.ds(CPITCH * (m + 1), 8, stride=CPITCH), :]
            h_ref[b, pl.ds(PITCH * m + 7, 8, stride=PITCH), :] = edge + first
            h_ref[b, pl.ds(PITCH * (m + 1), 8, stride=PITCH), :] = last + last


def local_terms(c):
    l = jnp.log2(1.0 + jnp.exp2(c * (1.5 * LOG2E) - 0.5 * LOG2E))
    return l * (W0 + l * (W1 + l * W2)), jnp.tanh(c), jnp.tanh(0.5 * c), jnp.exp2((c * c) * (-0.5 * LOG2E))


def values_tile(d_ref, h_ref, v_ref, e_refs):
    for b in range(2):
        cols = slice(128 * b, 128 * b + 128)
        for z in range(PLANES):
            m, n = z // 2, (z + 1) // 2
            at = PITCH * z + 8
            for g in range(0, 32, 8):
                near = h_ref[b, PITCH * m + 8 + g : PITCH * m + 16 + g, :]
                far = near if n == m else h_ref[b, PITCH * n + 8 + g : PITCH * n + 16 + g, :]
                c = d_ref[32 * z + g : 32 * z + g + 8, cols] + (near + far)
                v_ref[b, at + g : at + g + 8, :] = c
                if e_refs[b] is not None:
                    for i, term in enumerate(local_terms(c)):
                        e_refs[b][i, 32 * z + g : 32 * z + g + 8, :] = term
        for side, row in ((0, 7), (1, PITCH)):
            for odd in range(2):
                for m in range(0, 16, 8):
                    near = h_ref[b, pl.ds(PITCH * m + row, 8, stride=PITCH), :]
                    far = near if odd == 0 else h_ref[b, pl.ds(PITCH * (m + 1) + row, 8, stride=PITCH), :]
                    r = 1024 + 32 * side + 16 * odd + m
                    v_ref[b, pl.ds(PITCH * (2 * m + odd) + row, 8, stride=2 * PITCH), :] = d_ref[r : r + 8, cols] + (near + far)


def matmul_tile(a_ref, p_ref, at, d_ref):
    for r in (0, HALF):
        d_ref[r : r + HALF, :] = jnp.dot(a_ref[r : r + HALF, :], p_ref[at], preferred_element_type=F32)


def code(x, top):
    c = jnp.floor(jnp.log2(x) * STEPS + (top + 0.5))
    return jnp.minimum(jnp.maximum(c, -32768.0), 32767.0)


def march(trio, e_ref, groups):
    before, here, after = trio
    lane = lax.broadcasted_iota(jnp.int32, (8, 128), 1)
    first, last = lane == 0, lane == 127

    def load(of, g, z, off=0):
        at = PITCH * z + 8 + 8 * g + off
        return of[0][of[1], at : at + 8, :]

    zero = jnp.zeros((8, 128), F32)
    state = []
    for g in groups:
        c = load(here, g, 0)
        state.append((c, c, zero + 1.0, zero, zero, zero, zero))
    for z in range(PLANES):
        for at, g in enumerate(groups):
            prev, c, through, a0, a1, a2, a3 = state[at]
            following = load(here, g, z + 1) if z + 1 < PLANES else c
            xp = pltpu.roll(jnp.where(first, load(after, g, z), c), 127, 1)
            xm = pltpu.roll(jnp.where(last, load(before, g, z), c), 1, 1)
            dx = xp - xm
            dy = load(here, g, z, 1) - load(here, g, z, -1)
            dz = following - prev
            along = dx + (0.6 / 0.48) * dy + (0.64 / 0.48) * dz
            square = (4.0 + dx * dx) + (dy * dy + dz * dz)
            shading = 0.35 / GAIN + jnp.abs(along) * lax.rsqrt(square)
            absorbed, t1, t2, bell = (e_ref[i, 32 * z + 8 * g : 32 * z + 8 * g + 8, :] for i in range(4))
            weight = through * absorbed
            through = through - weight
            ws = weight * shading
            a0 = a0 + ws
            a1 = a1 + ws * t1
            a2 = a2 + ws * t2
            a3 = a3 + ws * bell
            state[at] = (c, following, through, a0, a1, a2, a3)
    return [one[2:] for one in state]


def march_half(trio, e_ref, o_ref, block, half):
    sets = []
    for through, a0, a1, a2, a3 in march(trio, e_ref, (2 * half, 2 * half + 1)):
        sets.append(
            (
                code((0.5 * GAIN) * (a0 + a1), COLOR_TOP),
                code((0.5 * GAIN) * (a0 - a2), COLOR_TOP),
                code(GAIN * a3, COLOR_TOP),
                code(-jnp.log2(through), TAU_TOP),
            )
        )
    for i in range(4):
        both = jnp.concatenate([sets[0][i], sets[1][i]], 0)
        o_ref[block, i, 16 * half : 16 * half + 16, :] = both.astype(jnp.int32).astype(jnp.int16)


def widening(w_ref):
    away = lax.broadcasted_iota(jnp.int32, (256, 256), 1) - 2 * lax.broadcasted_iota(jnp.int32, (256, 256), 0)
    w_ref[...] = jnp.where(away == 0, 0.25, jnp.where(jnp.abs(away) == 1, 0.125, 0.0)).astype(BF16)


def brick_kernel(a_hbm, above_hbm, below_hbm, coarse_hbm, lay_hbm, o_hbm, *scratch):
    a_ref, k_ref, w_ref, p_first, p_rest, d0, d1, d2, c0, c1, c2, h0, h1, h2, v0, v1, v2, v7 = scratch[:18]
    (e00, e01, e10, e11, e20, e21, e7), lay_ref, o_ref, sem, o_sem = scratch[18:25], *scratch[25:]
    cs, hs, ring, ds = (c0, c1, c2), (h0, h1, h2), (v0, v1, v2), (d0, d1, d2)
    es = ((e00, e01), (e10, e11), (e20, e21))
    copies = [
        pltpu.make_async_copy(of, to, sem.at[i])
        for i, (of, to) in enumerate(
            (
                (lay_hbm, lay_ref),
                (coarse_hbm, k_ref.at[pl.ds(0, 272)]),
                (above_hbm.at[:, pl.ds(2048, 1024)], k_ref.at[pl.ds(272, 32)]),
                (below_hbm.at[:, pl.ds(2048, 1024)], k_ref.at[pl.ds(304, 32)]),
                (above_hbm.at[:, pl.ds(0, 2048)], a_ref.at[pl.ds(1024, 32)]),
                (below_hbm.at[:, pl.ds(0, 2048)], a_ref.at[pl.ds(1056, 32)]),
                (a_hbm.at[:, pl.ds(0, 1024)], a_ref.at[pl.ds(0, 1024), pl.ds(0, 1024)]),
                (a_hbm.at[:, pl.ds(1024, 1024)], a_ref.at[pl.ds(0, 1024), pl.ds(1024, 1024)]),
            )
        )
    ]
    for copy in copies:
        copy.start()
    widening(w_ref)
    copies[0].wait()
    onehot(lay_ref, p_first, 0, TILES - 1)
    onehot(lay_ref, p_first, 1, 0)
    for copy in copies[1:4]:
        copy.wait()
    coarse_tile(TILES - 1, k_ref, w_ref, c2, h2)
    coarse_tile(0, k_ref, w_ref, c0, h0)
    for t in range(1, 7):
        onehot(lay_ref, p_rest, t - 1, t)
    for copy in copies[4:7]:
        copy.wait()
    for r in (0, HALF):
        d0[r : r + HALF, :] = jnp.dot(a_ref[r : r + HALF, :1024], p_first[0, :1024, :], preferred_element_type=F32)
    copies[7].wait()
    for r in (0, HALF):
        d0[r : r + HALF, :] += jnp.dot(a_ref[r : r + HALF, 1024:], p_first[0, 1024:, :], preferred_element_type=F32)
    matmul_tile(a_ref, p_first, 1, d1)
    values_tile(d0, h2, v7, (e7, None))
    values_tile(d0, h2, v2, (None, e21))
    matmul_tile(a_ref, p_rest, 0, d2)
    coarse_tile(1, k_ref, w_ref, c1, h1)
    values_tile(d1, h0, v0, es[0])

    def leave(block):
        return pltpu.make_async_copy(o_ref.at[block], o_hbm.at[block], o_sem.at[block])

    def trios(prev, cur):
        return ((prev, 0), (prev, 1), (cur, 0)), ((prev, 1), (cur, 0), (cur, 1))

    def three(i, _):
        for j in range(3):
            s = 3 * i + j

            @pl.when(i < 2)
            def _(j=j, s=s):
                before, after = (j + 2) % 3, (j + 1) % 3
                one, two = trios(ring[before], ring[j])
                block = 2 * s - 1 if j else jnp.where(i == 0, BLOCKS - 1, 2 * s - 1)
                values_tile(ds[before], hs[after], ring[after], es[after])
                coarse_tile(jnp.minimum(s + 2, 7), k_ref, w_ref, cs[before], hs[before])
                matmul_tile(a_ref, p_rest, jnp.minimum(s + 1, 5), ds[j])
                march_half(one, es[before][1], o_ref, block, 0)
                march_half(one, es[before][1], o_ref, block, 1)
                leave(block).start()
                march_half(two, es[j][0], o_ref, 2 * s, 0)
                march_half(two, es[j][0], o_ref, 2 * s, 1)
                leave(2 * s).start()

        return 0

    lax.fori_loop(0, 2, three, 0)
    for s, prev, cur, e_one, e_two in ((6, v2, v0, e21, e00), (7, v0, v7, e01, e7)):
        one, two = trios(prev, cur)
        for half in range(2):
            march_half(one, e_one, o_ref, 2 * s - 1, half)
        leave(2 * s - 1).start()
        for half in range(2):
            march_half(two, e_two, o_ref, 2 * s, half)
        leave(2 * s).start()
    for block in range(BLOCKS):
        leave(block).wait()


VMEM = pl.BlockSpec(memory_space=pltpu.VMEM)
ANY = pl.BlockSpec(memory_space=pl.ANY)


def brick(a, above, below, coarse, lay):
    return pl.pallas_call(
        brick_kernel,
        out_shape=jax.ShapeDtypeStruct((BLOCKS, 4, 32, 128), jnp.int16),
        in_specs=[ANY] * 5,
        out_specs=ANY,
        scratch_shapes=[
            pltpu.VMEM((1088, 2048), BF16),
            pltpu.VMEM((336, 1024), BF16),
            pltpu.VMEM((256, 256), BF16),
            pltpu.VMEM((2, 2048, 256), BF16),
            pltpu.VMEM((6, 2048, 256), BF16),
            *[pltpu.VMEM((1088, 256), F32)] * 3,
            *[pltpu.VMEM((2, 25 * CPITCH, 128), F32)] * 3,
            *[pltpu.VMEM((2, 25 * PITCH, 128), F32)] * 3,
            *[pltpu.VMEM((2, 33 * PITCH, 128), F32)] * 4,
            *[pltpu.VMEM((4, 1024, 128), F32)] * 7,
            pltpu.VMEM((8, 256), jnp.int32),
            pltpu.VMEM((BLOCKS, 4, 32, 128), jnp.int16),
            pltpu.SemaphoreType.DMA((8,)),
            pltpu.SemaphoreType.DMA((BLOCKS,)),
        ],
        compiler_params=pltpu.CompilerParams(vmem_limit_bytes=63 * 2**20),
        name="brick",
    )(a, above, below, coarse, lay)


def composite_kernel(order_ref, parts_ref, o_ref):
    flip = order_ref[0]

    def image(b, i):
        x = parts_ref[b, i].astype(jnp.int32).astype(F32)
        top = TAU_TOP if i == 3 else COLOR_TOP
        return jnp.where(x > -32768.0, jnp.exp2((x - top) * (1.0 / STEPS)), 0.0)

    tau = jnp.zeros((32, 128), F32)
    sums = [jnp.zeros((32, 128), F32) for _ in range(3)]
    for rank in range(BLOCKS):
        b = rank ^ flip
        passing = jnp.exp2(-tau)
        for i in range(3):
            sums[i] = sums[i] + passing * image(b, i)
        tau = tau + image(b, 3)
    for i in range(3):
        o_ref[i] = sums[i]
    o_ref[3] = 1.0 - jnp.exp2(-tau)


def composite(order, parts):
    return pl.pallas_call(
        composite_kernel,
        out_shape=jax.ShapeDtypeStruct((4, 32, 128), F32),
        in_specs=[pl.BlockSpec(memory_space=pltpu.SMEM), VMEM],
        out_specs=VMEM,
        name="composite",
    )(order, parts)


def edge(detail, coarse, row, crow):
    lines = detail[:, row, :]
    fine = jnp.concatenate([lines[0::2], lines[1::2]], 0)
    rough = jnp.pad(coarse[:, crow, :], ((0, 15), (0, 0)))
    return jnp.concatenate([fine, rough], 1)


def on_device(coarse, detail, layout, view_order):
    n = lax.axis_size("rows")
    above = lax.ppermute(edge(detail, coarse, 31, 15), "rows", [(i, (i + 1) % n) for i in range(n)])
    below = lax.ppermute(edge(detail, coarse, 0, 0), "rows", [((i + 1) % n, i) for i in range(n)])
    codes = brick(detail.reshape(1024, 2048), above, below, coarse.reshape(272, 1024), layout.reshape(8, 256))
    parts = lax.all_to_all(codes, "depth", 0, 0, tiled=True)
    return composite(view_order, parts)


def solution(mesh):
    in_specs = (P("depth", "rows", None), P("depth", "rows", None), P(), P())
    out_specs = P(None, "rows", "depth")
    return jax.shard_map(on_device, mesh=mesh, in_specs=in_specs, out_specs=out_specs, check_vma=False)
```
